32 devices in a mesh: rep: 2 (over x), seq: 4 (over y, core), dp: 4 (over z).
Axes of the slice: x: 2, y: 2, z: 4, core: 2. Of those that a mesh axis runs over, the one named last changes fastest.
Arguments:
- queries: bfloat16 [8, 1024, 2048], P(('rep', 'dp'), 'seq'), parts along dimension 0, may hold values from -20 to 20
- keys: bfloat16 [8, 1024, 2048], P(('rep', 'dp'), 'seq'), parts along dimension 0, may hold values from -20 to 20
- values: bfloat16 [8, 1024, 2048], P(('rep', 'dp'), 'seq'), parts along dimension 0, may hold values from -6 to 6
- lengths: int32 [8, 8], P(('rep', 'dp')), parts along dimension 0, may hold values from 1 to 512, 1024 in all within a row
Outputs:
- attended: bfloat16 [8, 1024, 2048], P(('rep', 'dp'), 'seq'), parts along dimension 0
- doc_vectors: float32 [8, 8, 2048], P(('rep', 'dp')), parts along dimension 0
The draws below stay inside these ranges and needn't reach their ends.
There are 2 independent parts, one for each index of `rep`. The reference program is written for one: setup_inputs(seed, part) draws one part's arguments, and reference() takes and returns one part's arrays. A program takes and returns all parts, laid end to end along the dimension named above; each array names one. Nothing has to cross between parts.
Inputs may be any that keep to these rules, and one draw needn't show every extreme that they name: Each row holds 8 lengths that sum to 1024, and its largest is 512.
All inputs are finite; a program needn't handle non-finite values.
Results may differ from the reference program's by a relative error of at most 0.0051.
Values may be sent and summed in bfloat16 or wider, within the bound.
A program may use at most 64 MiB of HBM per device.

```python
import math
import jax
import jax.numpy as jnp
import numpy as np
from jax import lax

HEADS = 16
HD = 128
NDOC = 8
HW = 2048
STREAM = 1024
MOST = 512
GROUPS = 4


def draw_queries(key, part):
    key = jax.random.fold_in(key, 11)
    return (2.0 * jax.random.truncated_normal(key, -6.0, 6.0, (GROUPS, STREAM, HW), jnp.float32)).astype(jnp.bfloat16)


def draw_keys(key, part):
    key = jax.random.fold_in(key, 12)
    return jax.random.truncated_normal(key, -6.0, 6.0, (GROUPS, STREAM, HW), jnp.float32).astype(jnp.bfloat16)


def steps_of(own_key, shape, cuts, low, top_value):
    factor_of = 1.0
    for position, parts in cuts:
        steps = jax.random.uniform(jax.random.fold_in(jax.random.fold_in(own_key, 6), position), (parts,), jnp.float32, low / len(cuts), top_value / len(cuts))
        factor_of = factor_of * jnp.repeat(jnp.exp(steps), shape[position] // parts).reshape((-1,) + (1,) * (len(shape) - 1 - position))
    return factor_of


def split_up(amount, total, most, skew):
    loads = [(1 << 20) // math.isqrt(standing ** skew) + 1 for standing in range(2, amount + 1)]
    surplus, counts = total - most - (amount - 1), [1] * (amount - 1)
    while surplus > 0:
        movable = [i for i in range(amount - 1) if counts[i] < most]
        mass, left = sum([loads[i] for i in movable]), surplus
        for i in movable:
            more = min(most - counts[i], max(1, left * loads[i] // mass), surplus)
            counts[i] = counts[i] + more
            surplus = surplus - more
    return np.array([most] + counts)


def ragged(rng, number_of, total, bound, skew):
    if number_of == 2:
        one = jax.random.randint(rng, (), max(1, total - bound), min(bound, total - 1) + 1)
        return jnp.stack([one, total - one])
    sizes = jnp.asarray(split_up(number_of, total, bound, skew), jnp.int32)
    pairs = (number_of - 1) // 2
    source_of, taker = sizes[1:1 + 2 * pairs:2], sizes[2:2 + 2 * pairs:2]
    room = jnp.minimum(source_of - 1, bound - taker)
    passed = jax.random.randint(jax.random.fold_in(rng, 1), (pairs,), 0, 1 << 20) % (room + 1)
    sizes = sizes.at[1:1 + 2 * pairs:2].set(source_of - passed).at[2:2 + 2 * pairs:2].set(taker + passed)
    return sizes[jax.random.permutation(jax.random.fold_in(rng, 2), number_of)]


def gaussian(own_key, extent, spread, bound, pieces=(), kind=jnp.bfloat16):
    result = jax.random.normal(own_key, extent, jnp.float32) * spread
    if len(pieces) > 0:
        result = steps_of(own_key, extent, pieces, -0.22, 0.18) * result
    return jnp.clip(result, min=-bound, max=bound).astype(kind)


def setup_inputs(seed: int = 0, part: int = 0) -> dict:
    key_of = jax.random.split(jax.random.key(seed), 5)
    own_keys = jax.random.split(jax.random.fold_in(key_of[4], part), 5)
    return {
        "queries": draw_queries(jax.random.fold_in(jax.random.fold_in(key_of[4], part), 71), part),
        "keys": draw_keys(jax.random.fold_in(jax.random.fold_in(key_of[4], part), 71), part),
        "values": gaussian(own_keys[2], (GROUPS, STREAM, HW), 1.0, 6.0, ((0, 4), (1, 4))),
        "lengths": jax.vmap(lambda own: ragged(own, NDOC, STREAM, MOST, 2))(jax.random.split(own_keys[3], GROUPS)).reshape((GROUPS, NDOC)).astype(jnp.int32),
    }


def doc_index(lens, positions):
    ends = jnp.cumsum(lens).astype(jnp.int32)
    return lax.optimization_barrier(jnp.sum((ends[None, :] <= positions[:, None]).astype(jnp.int32), axis=1)).astype(jnp.int32)

def attend(queries_h, keys_h, values_h, doc_ids):
    stream = queries_h.shape[0]
    block = 512 if stream % 512 == 0 else stream
    count = stream // block
    scale = 1.0 / queries_h.shape[2] ** 0.5

    def one_block(index):
        start = (index * block).astype(jnp.int32)
        q_block = lax.dynamic_slice_in_dim(queries_h, start, block, 0)
        ids = lax.dynamic_slice_in_dim(doc_ids, start, block, 0)
        scores = jnp.einsum('qhd,khd->hqk', q_block.astype(jnp.float32), keys_h.astype(jnp.float32)) * scale
        same = ids[:, None] == doc_ids[None, :]
        scores = jnp.where(same[None], scores, -1e+30)
        top = lax.optimization_barrier(jnp.max(scores, axis=2, keepdims=True))
        expo = jnp.exp(scores - top)
        probs = expo / lax.optimization_barrier(jnp.sum(expo, axis=2, keepdims=True))
        weights = probs.astype(jnp.bfloat16)
        mixed = jnp.einsum('hqk,khd->qhd', weights.astype(jnp.float32), values_h.astype(jnp.float32), precision=lax.Precision.HIGHEST)
        return mixed.astype(jnp.bfloat16)
    out = lax.map(one_block, jnp.arange(count, dtype=jnp.int32))
    return out.reshape(stream, queries_h.shape[1], queries_h.shape[2])

def normalize(sums):
    return sums / jnp.sqrt(lax.optimization_barrier(jnp.mean(sums * sums, axis=-1, keepdims=True)) + 1e-06)

def reference(queries, keys, values, lengths):

    def column(items):
        q_col, k_col, v_col, lens = items
        ids = doc_index(lens, jnp.arange(STREAM, dtype=jnp.int32))
        out = attend(q_col.reshape(STREAM, HEADS, HD), k_col.reshape(STREAM, HEADS, HD), v_col.reshape(STREAM, HEADS, HD), ids)
        rows = out.reshape(STREAM, HEADS * HD)
        onehot = (ids[None, :] == jnp.arange(NDOC, dtype=jnp.int32)[:, None]).astype(jnp.bfloat16)
        sums = jnp.dot(onehot, rows, preferred_element_type=jnp.float32)
        return (rows, normalize(sums))
    attended, doc_vectors = lax.map(column, (queries, keys, values, lengths))
    return (attended, doc_vectors)
```

```python
import jax
import jax.numpy as jnp
from jax import lax
from jax.experimental import pallas as pl
from jax.experimental.pallas import tpu as pltpu
from jax.sharding import PartitionSpec as P

HEADS = 16
HD = 128


def doc_index(lens, positions):
    ends = jnp.cumsum(lens)
    return jnp.sum((ends[None, :] <= positions[:, None]).astype(jnp.int32), axis=1)


def attend(queries_h, keys_h, values_h, doc_ids):
    stream = queries_h.shape[0]
    block = 512
    count = stream // block
    scale = 1.0 / queries_h.shape[2] ** 0.5

    def one_block(index):
        start = index * block
        q_block = lax.dynamic_slice_in_dim(queries_h, start, block, 0)
        ids = lax.dynamic_slice_in_dim(doc_ids, start, block, 0)
        scores = (
            jnp.einsum("qhd,khd->hqk", q_block, keys_h, preferred_element_type=jnp.float32) * scale
        )
        same = ids[:, None] == doc_ids[None, :]
        scores = jnp.where(same[None], scores, -1e30)
        top = jnp.max(scores, axis=2, keepdims=True)
        expo = jnp.exp(scores - top)
        probs = expo / jnp.sum(expo, axis=2, keepdims=True)
        weights = probs.astype(jnp.bfloat16)
        mixed = jnp.einsum("hqk,khd->qhd", weights, values_h, preferred_element_type=jnp.float32)
        return mixed.astype(jnp.bfloat16)

    out = lax.map(one_block, jnp.arange(count, dtype=jnp.int32))
    return out.reshape(stream, queries_h.shape[1], queries_h.shape[2])


def normalize(sums):
    return sums / jnp.sqrt(jnp.mean(sums * sums, axis=-1, keepdims=True) + 1e-06)


def any_axis(queries, keys, values, lengths):
    members = lax.axis_size("seq")
    tok_rows = queries.shape[1]
    width = queries.shape[2]
    local_heads = HEADS // members
    group_width = local_heads * HD
    stream = tok_rows * members
    lens = lengths[0]
    doc_count = lens.shape[0]
    q_split = queries[0].reshape(tok_rows, members, group_width)
    k_split = keys[0].reshape(tok_rows, members, group_width)
    v_split = values[0].reshape(tok_rows, members, group_width)
    q_heads, k_heads, v_heads = (
        lax.all_to_all(q_split, "seq", split_axis=1, concat_axis=0, tiled=True),
        lax.all_to_all(k_split, "seq", split_axis=1, concat_axis=0, tiled=True),
        lax.all_to_all(v_split, "seq", split_axis=1, concat_axis=0, tiled=True),
    )
    all_ids = doc_index(lens, jnp.arange(stream, dtype=jnp.int32))
    head_out = attend(
        q_heads.reshape(stream, local_heads, HD),
        k_heads.reshape(stream, local_heads, HD),
        v_heads.reshape(stream, local_heads, HD),
        all_ids,
    )
    head_rows = head_out.reshape(stream, 1, group_width)
    back = lax.all_to_all(head_rows, "seq", split_axis=0, concat_axis=1, tiled=True)
    rows = back.reshape(tok_rows, width)
    doc_range = jnp.arange(doc_count, dtype=jnp.int32)
    start = lax.axis_index("seq") * tok_rows
    local_ids = doc_index(lens, start + jnp.arange(tok_rows, dtype=jnp.int32))
    onehot_local = (local_ids[None, :] == doc_range[:, None]).astype(jnp.bfloat16)
    token_part = jnp.dot(onehot_local, rows, preferred_element_type=jnp.float32)
    sums = lax.psum(token_part, "seq")
    return (rows.reshape(1, tok_rows, width), normalize(sums).reshape(1, doc_count, width))


NEG = -1e30
LOG2E = 1.4426950408889634
MESH = pl.DeviceIdType.MESH


def pair_kernel(
    lens_ref, q_hbm, k_hbm, v_hbm, out_hbm, dv_ref,
    q_all, k_all, v_all, bias, send, recv, stat_send, stat_recv,
    local_out, local_lse, final, sums, peer_sums,
    own_sem, sib_send, sib_recv, msg_send, msg_recv, st_send, st_recv,
    out_own, out_send, out_recv, sum_send, sum_recv,
):
    me = lax.axis_index("seq")
    chip = me // 2
    core = lax.rem(me, 2)
    sibling = chip * 2 + 1 - core
    partner = (1 - chip) * 2 + core
    diagonal = (1 - chip) * 2 + 1 - core
    tok = q_hbm.shape[1]
    rows = 2 * tok
    half = q_hbm.shape[2] // 2
    heads = half // HD
    docs = lens_ref.shape[1]
    factor = LOG2E / HD**0.5
    blocks = rows // 128

    def column(h):
        return pl.ds(pl.multiple_of(h * HD, HD), HD)

    def group(g):
        return pl.ds(pl.multiple_of(g * half, half), half)

    def span(c):
        return pl.ds(pl.multiple_of(c * tok, tok), tok)

    own_copies = [
        pltpu.make_async_copy(src.at[0, :, group(core)], dst.at[span(core), :], own_sem.at[i])
        for i, (src, dst) in enumerate(((q_hbm, q_all), (k_hbm, k_all), (v_hbm, v_all)))
    ]
    for copy in own_copies:
        copy.start()

    barrier = pltpu.get_barrier_semaphore()
    for other in (sibling, partner, diagonal):
        pl.semaphore_signal(barrier, inc=1, device_id={"seq": other}, device_id_type=MESH)
    pl.semaphore_wait(barrier, 3)

    sib_copies = [
        pltpu.make_async_remote_copy(
            src_ref=src.at[0, :, group(1 - core)], dst_ref=dst.at[span(core), :],
            send_sem=sib_send.at[i], recv_sem=sib_recv.at[i],
            device_id={"seq": sibling}, device_id_type=MESH,
        )
        for i, (src, dst) in enumerate(((q_hbm, q_all), (k_hbm, k_all), (v_hbm, v_all)))
    ]
    for copy in sib_copies:
        copy.start()

    ends = []
    total = jnp.int32(0)
    for j in range(docs):
        total = total + lens_ref[0, j]
        ends.append(total)
    first = jnp.int32(0)
    last = jnp.int32(2 * rows)
    for end in ends:
        first = jnp.maximum(first, jnp.where(end <= rows, end, 0))
        last = jnp.minimum(last, jnp.where(end > rows, end, 2 * rows))
    low = jnp.where(chip == 0, first, 0)
    high = jnp.where(chip == 0, rows, last - rows)

    def in_cross(index):
        return (index >= low) & (index < high)

    def message(t, source):
        return pltpu.make_async_remote_copy(
            src_ref=source, dst_ref=recv.at[t],
            send_sem=msg_send.at[t], recv_sem=msg_recv.at[t],
            device_id={"seq": partner}, device_id_type=MESH,
        )

    def stats(h):
        return pltpu.make_async_remote_copy(
            src_ref=stat_send.at[h], dst_ref=stat_recv.at[h],
            send_sem=st_send.at[h], recv_sem=st_recv.at[h],
            device_id={"seq": partner}, device_id_type=MESH,
        )

    own_copies[0].wait()
    sib_copies[0].wait_recv()
    for t in range(2):
        message(t, q_all.at[:, t * HD : (t + 1) * HD]).start()

    def ids_of(index):
        ids = jnp.zeros(index.shape, jnp.int32)
        for end in ends:
            ids = ids + (end <= index).astype(jnp.int32)
        return ids

    lane_pos = lax.broadcasted_iota(jnp.int32, (1, rows), 1)
    lane_ids = ids_of(lane_pos + chip * rows)
    sub_ids = ids_of(lax.broadcasted_iota(jnp.int32, (rows, 1), 0) + chip * rows)
    bias[...] = jnp.where(sub_ids == lane_ids, 0.0, NEG)
    cross_bias = jnp.where(in_cross(lane_pos), 0.0, NEG)
    onehot = (lane_ids == lax.broadcasted_iota(jnp.int32, (docs, rows), 0)).astype(jnp.bfloat16)
    eye = lax.broadcasted_iota(jnp.int32, (128, 128), 0) == lax.broadcasted_iota(
        jnp.int32, (128, 128), 1
    )
    ones = jnp.ones((rows, HD), jnp.bfloat16)
    chunk = min(CHUNK, rows)

    for i in (1, 2):
        own_copies[i].wait()
        sib_copies[i].wait_recv()

    def mix(q, h, bias_rows):
        scores = lax.dot_general(
            q, k_all[:, column(h)], (((1,), (1,)), ((), ())), preferred_element_type=jnp.float32
        )
        scores = scores * factor + bias_rows
        top = jnp.max(scores, axis=1, keepdims=True)
        expo = jnp.exp2(scores - top).astype(jnp.bfloat16)
        wide = jnp.concatenate([v_all[:, column(h)], ones], axis=1)
        both = jnp.dot(expo, wide, preferred_element_type=jnp.float32)
        mass = both[:, HD:]
        return both[:, :HD] / mass, top + jnp.log2(mass)

    def local(h):
        for start in range(0, rows, chunk):
            part = slice(start, start + chunk)
            out, lse = mix(q_all[part, column(h)], h, bias[part, :])
            local_out[h, part, :] = out
            local_lse[h, part, :] = lse

    def remote(h, with_query):
        t = h + 2
        message(h, send.at[h]).wait_recv()
        for start in range(0, rows, chunk):
            part = slice(start, start + chunk)
            out, lse = mix(recv[h, part, :], h, cross_bias)
            out = out.astype(jnp.bfloat16)
            if with_query:
                index = start + lax.broadcasted_iota(jnp.int32, (chunk, HD), 0)
                out = jnp.where(in_cross(index), q_all[part, column(t)].astype(jnp.float32), out.astype(jnp.float32)).astype(jnp.bfloat16)
            send[t, part, :] = out
            for i in range(chunk // 128):
                block = jnp.where(eye, lse[i * 128 : (i + 1) * 128, :], 0.0)
                at = start // 128 + i
                stat_send[h, at : at + 1, :] = jnp.sum(block, axis=0, keepdims=True)
        message(t, send.at[t]).start()
        stats(h).start()

    def out_copy(h):
        where = pl.ds(pl.multiple_of(core * half + h * HD, HD), HD)
        keep = pltpu.make_async_copy(
            final.at[h, span(core), :], out_hbm.at[0, :, where], out_own.at[h]
        )
        give = pltpu.make_async_remote_copy(
            src_ref=final.at[h, span(1 - core), :], dst_ref=out_hbm.at[0, :, where],
            send_sem=out_send.at[h], recv_sem=out_recv.at[h],
            device_id={"seq": sibling}, device_id_type=MESH,
        )
        return keep, give

    def combine(h):
        stats(h).wait_recv()
        for i in range(blocks):
            part = slice(i * 128, (i + 1) * 128)
            line = jnp.broadcast_to(stat_recv[h, i : i + 1, :], (128, 128))
            other = jnp.sum(jnp.where(eye, line, 0.0), axis=1, keepdims=True)
            index = i * 128 + lax.broadcasted_iota(jnp.int32, (128, HD), 0)
            gap = jnp.where(in_cross(index), local_lse[h, part, :] - other, 200.0)
            share = 1.0 / (1.0 + jnp.exp2(jnp.minimum(gap, 100.0)))
            share = jnp.where(gap > 99.0, 0.0, share)
            mine = local_out[h, part, :]
            theirs = recv[h + 2, part, :].astype(jnp.float32)
            final[h, part, :] = (mine + share * (theirs - mine)).astype(jnp.bfloat16)
        for copy in out_copy(h):
            copy.start()
        sums[:, column(h)] = jnp.dot(onehot, final[h], preferred_element_type=jnp.float32)

    def loop(begin, end, body):
        def step(h, carry):
            body(h)
            return carry

        lax.fori_loop(begin, end, step, 0)

    def opening(h):
        remote(h, True)
        local(h + 2)

    def middle(h):
        remote(h, True)
        local(h + 2)
        combine(h - 2)

    def closing(h):
        remote(h, False)
        combine(h - 2)

    loop(0, 2, local)
    loop(0, 2, opening)
    loop(2, heads - 2, middle)
    loop(heads - 2, heads, closing)
    for h in (heads - 2, heads - 1):
        message(h + 2, send.at[h + 2]).wait_recv()
        combine(h)

    sum_copies = [
        pltpu.make_async_remote_copy(
            src_ref=sums, dst_ref=peer_sums.at[i],
            send_sem=sum_send.at[i], recv_sem=sum_recv.at[i],
            device_id={"seq": other}, device_id_type=MESH,
        )
        for i, other in enumerate((partner, sibling, diagonal))
    ]
    for copy in sum_copies:
        copy.start()

    for copy in sib_copies:
        copy.wait_send()

    def finish(t):
        message(t, send.at[t]).wait_send()

    loop(0, heads + 2, finish)

    def finish_head(h):
        stats(h).wait_send()
        keep, give = out_copy(h)
        keep.wait()
        give.wait_send()
        give.wait_recv()

    loop(0, heads, finish_head)
    for copy in sum_copies:
        copy.wait()
    here = sums[...] + peer_sums[0]
    there = peer_sums[1] + peer_sums[2]
    square = jnp.sum(here * here, axis=1, keepdims=True) + jnp.sum(
        there * there, axis=1, keepdims=True
    )
    root = jnp.sqrt(square / (2 * half) + 1e-06)
    dv_ref[0, :, group(core)] = here / root
    dv_ref[0, :, group(1 - core)] = there / root


CHUNK = 256


def two_chips(queries, keys, values, lengths):
    _, tok, width = queries.shape
    rows, half, docs = 2 * tok, width // 2, lengths.shape[1]
    heads = half // HD
    bf, f32 = jnp.bfloat16, jnp.float32
    dma = pltpu.SemaphoreType.DMA
    hbm = pl.BlockSpec(memory_space=pl.ANY)
    return pl.pallas_call(
        pair_kernel,
        out_shape=(
            jax.ShapeDtypeStruct(queries.shape, bf),
            jax.ShapeDtypeStruct((1, docs, width), f32),
        ),
        in_specs=[pl.BlockSpec(memory_space=pltpu.SMEM), hbm, hbm, hbm],
        out_specs=(hbm, pl.BlockSpec(memory_space=pltpu.VMEM)),
        scratch_shapes=[
            pltpu.VMEM((rows, half), bf),
            pltpu.VMEM((rows, half), bf),
            pltpu.VMEM((rows, half), bf),
            pltpu.VMEM((rows, rows), f32),
            pltpu.VMEM((heads + 2, rows, HD), bf),
            pltpu.VMEM((heads + 2, rows, HD), bf),
            pltpu.VMEM((heads, max(rows // 128, 8), 128), f32),
            pltpu.VMEM((heads, max(rows // 128, 8), 128), f32),
            pltpu.VMEM((heads, rows, HD), f32),
            pltpu.VMEM((heads, rows, HD), f32),
            pltpu.VMEM((heads, rows, HD), bf),
            pltpu.VMEM((docs, half), f32),
            pltpu.VMEM((3, docs, half), f32),
            dma((3,)), dma((3,)), dma((3,)),
            dma((heads + 2,)), dma((heads + 2,)),
            dma((heads,)), dma((heads,)),
            dma((heads,)), dma((heads,)), dma((heads,)),
            dma((3,)), dma((3,)),
        ],
        compiler_params=pltpu.CompilerParams(
            collective_id=0, has_side_effects=True, vmem_limit_bytes=48 * 1024 * 1024
        ),
        cost_estimate=pl.CostEstimate(
            flops=8 * heads * rows * rows * HD, bytes_accessed=8 * tok * width,
            transcendentals=2 * heads * rows * rows,
        ),
    )(lengths, queries, keys, values)


def per_device(queries, keys, values, lengths):
    if lax.axis_size("seq") == 4:
        return two_chips(queries, keys, values, lengths)
    return any_axis(queries, keys, values, lengths)


def solution(mesh):
    return jax.shard_map(
        per_device,
        mesh=mesh,
        in_specs=(
            P(("rep", "dp"), "seq", None),
            P(("rep", "dp"), "seq", None),
            P(("rep", "dp"), "seq", None),
            P(("rep", "dp"), None),
        ),
        out_specs=(P(("rep", "dp"), "seq", None), P(("rep", "dp"), None, None)),
        check_vma=False,
    )
```

```python
import jax
import jax.numpy as jnp
from jax import lax
from jax.experimental import pallas as pl
from jax.experimental.pallas import tpu as pltpu
from jax.sharding import PartitionSpec as P

HEADS = 16
HD = 128


def doc_index(lens, positions):
    ends = jnp.cumsum(lens)
    return jnp.sum((ends[None, :] <= positions[:, None]).astype(jnp.int32), axis=1)


def attend(queries_h, keys_h, values_h, doc_ids):
    stream = queries_h.shape[0]
    block = 512
    count = stream // block
    scale = 1.0 / queries_h.shape[2] ** 0.5

    def one_block(index):
        start = index * block
        q_block = lax.dynamic_slice_in_dim(queries_h, start, block, 0)
        ids = lax.dynamic_slice_in_dim(doc_ids, start, block, 0)
        scores = (
            jnp.einsum("qhd,khd->hqk", q_block, keys_h, preferred_element_type=jnp.float32) * scale
        )
        same = ids[:, None] == doc_ids[None, :]
        scores = jnp.where(same[None], scores, -1e30)
        top = jnp.max(scores, axis=2, keepdims=True)
        expo = jnp.exp(scores - top)
        probs = expo / jnp.sum(expo, axis=2, keepdims=True)
        weights = probs.astype(jnp.bfloat16)
        mixed = jnp.einsum("hqk,khd->qhd", weights, values_h, preferred_element_type=jnp.float32)
        return mixed.astype(jnp.bfloat16)

    out = lax.map(one_block, jnp.arange(count, dtype=jnp.int32))
    return out.reshape(stream, queries_h.shape[1], queries_h.shape[2])


def normalize(sums):
    return sums / jnp.sqrt(jnp.mean(sums * sums, axis=-1, keepdims=True) + 1e-06)


def any_axis(queries, keys, values, lengths):
    members = lax.axis_size("seq")
    tok_rows = queries.shape[1]
    width = queries.shape[2]
    local_heads = HEADS // members
    group_width = local_heads * HD
    stream = tok_rows * members
    lens = lengths[0]
    doc_count = lens.shape[0]
    q_split = queries[0].reshape(tok_rows, members, group_width)
    k_split = keys[0].reshape(tok_rows, members, group_width)
    v_split = values[0].reshape(tok_rows, members, group_width)
    q_heads, k_heads, v_heads = (
        lax.all_to_all(q_split, "seq", split_axis=1, concat_axis=0, tiled=True),
        lax.all_to_all(k_split, "seq", split_axis=1, concat_axis=0, tiled=True),
        lax.all_to_all(v_split, "seq", split_axis=1, concat_axis=0, tiled=True),
    )
    all_ids = doc_index(lens, jnp.arange(stream, dtype=jnp.int32))
    head_out = attend(
        q_heads.reshape(stream, local_heads, HD),
        k_heads.reshape(stream, local_heads, HD),
        v_heads.reshape(stream, local_heads, HD),
        all_ids,
    )
    head_rows = head_out.reshape(stream, 1, group_width)
    back = lax.all_to_all(head_rows, "seq", split_axis=0, concat_axis=1, tiled=True)
    rows = back.reshape(tok_rows, width)
    doc_range = jnp.arange(doc_count, dtype=jnp.int32)
    start = lax.axis_index("seq") * tok_rows
    local_ids = doc_index(lens, start + jnp.arange(tok_rows, dtype=jnp.int32))
    onehot_local = (local_ids[None, :] == doc_range[:, None]).astype(jnp.bfloat16)
    token_part = jnp.dot(onehot_local, rows, preferred_element_type=jnp.float32)
    sums = lax.psum(token_part, "seq")
    return (rows.reshape(1, tok_rows, width), normalize(sums).reshape(1, doc_count, width))


NEG = -1e30
LOG2E = 1.4426950408889634
MESH = pl.DeviceIdType.MESH


def pair_kernel(
    lens_hbm, q_hbm, k_hbm, v_hbm, out_hbm, dv_ref,
    lens, q_all, k_all, v_all, bias, send, recv, stat_send, stat_recv,
    local_out, local_lse, final, expo_last, top_last, sums, peer_sums,
    lens_sem, own_sem, sib_send, sib_recv, early_send, early_recv, msg_send, msg_recv,
    st_send, st_recv, out_own, out_send, out_recv, sum_send, sum_recv,
):
    me = lax.axis_index("seq")
    chip = me // 2
    core = lax.rem(me, 2)
    sibling = chip * 2 + 1 - core
    partner = (1 - chip) * 2 + core
    diagonal = (1 - chip) * 2 + 1 - core
    tok = q_hbm.shape[1]
    rows = 2 * tok
    half = q_hbm.shape[2] // 2
    heads = half // HD
    docs = lens.shape[1]
    factor = LOG2E / HD**0.5
    pieces = rows // PIECE
    blocks = PIECE // 128

    def column(h):
        return pl.ds(pl.multiple_of(h * HD, HD), HD)

    def group(g):
        return pl.ds(pl.multiple_of(g * half, half), half)

    def span(c):
        return pl.ds(pl.multiple_of(c * tok, tok), tok)

    lens_copy = pltpu.make_async_copy(lens_hbm, lens, lens_sem)
    lens_copy.start()
    own_copies = [
        pltpu.make_async_copy(src.at[0, :, group(core)], dst.at[span(core), :], own_sem.at[i])
        for i, (src, dst) in enumerate(((k_hbm, k_all), (v_hbm, v_all), (q_hbm, q_all)))
    ]
    for copy in own_copies:
        copy.start()

    barrier = pltpu.get_barrier_semaphore()
    for other in (sibling, partner, diagonal):
        pl.semaphore_signal(barrier, inc=1, device_id={"seq": other}, device_id_type=MESH)
    pl.semaphore_wait(barrier, 3)

    def early(t, i, there, g):
        return pltpu.make_async_remote_copy(
            src_ref=q_hbm.at[0, :, pl.ds(pl.multiple_of(g * half + t * HD, HD), HD)],
            dst_ref=recv.at[t, span(core), :],
            send_sem=early_send.at[t, i], recv_sem=early_recv.at[t, core],
            device_id={"seq": there}, device_id_type=MESH,
        )

    early_copies = [
        early(t, i, *to) for t in range(2) for i, to in enumerate(((partner, core), (diagonal, 1 - core)))
    ]
    for copy in early_copies:
        copy.start()
    sib_copies = [
        pltpu.make_async_remote_copy(
            src_ref=src.at[0, :, group(1 - core)], dst_ref=dst.at[span(core), :],
            send_sem=sib_send.at[i], recv_sem=sib_recv.at[i],
            device_id={"seq": sibling}, device_id_type=MESH,
        )
        for i, (src, dst) in enumerate(((k_hbm, k_all), (v_hbm, v_all), (q_hbm, q_all)))
    ]
    for copy in sib_copies:
        copy.start()

    lens_copy.wait()
    ends = []
    total = jnp.int32(0)
    for j in range(docs):
        total = total + lens[0, j]
        ends.append(total)
    first = jnp.int32(0)
    last = jnp.int32(2 * rows)
    for end in ends:
        first = jnp.maximum(first, jnp.where(end <= rows, end, 0))
        last = jnp.minimum(last, jnp.where(end > rows, end, 2 * rows))
    low = jnp.where(chip == 0, first, 0)
    high = jnp.where(chip == 0, rows, last - rows)

    other_low = jnp.where(chip == 0, 0, first)
    other_high = jnp.where(chip == 0, last - rows, rows)

    def in_cross(index):
        return (index >= low) & (index < high)

    def ids_of(index):
        ids = jnp.zeros(index.shape, jnp.int32)
        for end in ends:
            ids = ids + (end <= index).astype(jnp.int32)
        return ids

    lane_pos = lax.broadcasted_iota(jnp.int32, (1, rows), 1)
    lane_ids = ids_of(lane_pos + chip * rows)
    sub_ids = ids_of(lax.broadcasted_iota(jnp.int32, (rows, 1), 0) + chip * rows)
    bias[...] = jnp.where(sub_ids == lane_ids, 0.0, NEG)
    cross_bias = jnp.where(in_cross(lane_pos), 0.0, NEG)
    other_bias = jnp.where((lane_pos >= other_low) & (lane_pos < other_high), 0.0, NEG)
    onehot = (lane_ids == lax.broadcasted_iota(jnp.int32, (docs, rows), 0)).astype(jnp.bfloat16)
    eye = lax.broadcasted_iota(jnp.int32, (128, 128), 0) == lax.broadcasted_iota(
        jnp.int32, (128, 128), 1
    )
    ones = jnp.ones((rows, HD), jnp.bfloat16)

    def part_of(p):
        return slice(p * PIECE, (p + 1) * PIECE)

    def message(t, p):
        return pltpu.make_async_remote_copy(
            src_ref=send.at[t, part_of(p), :], dst_ref=recv.at[t, part_of(p), :],
            send_sem=msg_send.at[t, p], recv_sem=msg_recv.at[t, p],
            device_id={"seq": partner}, device_id_type=MESH,
        )

    def stats(h):
        return pltpu.make_async_remote_copy(
            src_ref=stat_send.at[h], dst_ref=stat_recv.at[h],
            send_sem=st_send.at[h], recv_sem=st_recv.at[h],
            device_id={"seq": partner}, device_id_type=MESH,
        )

    def expo_of(q, keys, bias_rows):
        scores = lax.dot_general(
            q, keys, (((1,), (1,)), ((), ())), preferred_element_type=jnp.float32
        )
        scores = scores * factor + bias_rows
        top = jnp.max(scores, axis=1, keepdims=True)
        return jnp.exp2(scores - top).astype(jnp.bfloat16), top

    def weigh(expo, top, vals):
        wide = jnp.concatenate([vals, ones], axis=1)
        both = jnp.dot(expo, wide, preferred_element_type=jnp.float32)
        mass = both[:, HD:]
        return both[:, :HD] / mass, top + jnp.log2(mass)

    def mix(q, h, bias_rows):
        expo, top = expo_of(q, k_all[:, column(h)], bias_rows)
        return weigh(expo, top, v_all[:, column(h)])

    def local(h, p):
        part = part_of(p)
        out, lse = mix(q_all[part, column(h)], h, bias[part, :])
        local_out[h, part, :] = out
        local_lse[h, part, :] = lse

    def remote(h, p, source, at):
        part = part_of(p)
        out, lse = mix(recv[h, part, :], h, cross_bias)
        index = p * PIECE + lax.broadcasted_iota(jnp.int32, (PIECE, HD), 0)
        own = source[part, column(at)].astype(jnp.float32)
        send[h + 2, part, :] = jnp.where(in_cross(index), own, out).astype(jnp.bfloat16)
        message(h + 2, p).start()
        for i in range(blocks):
            block = jnp.where(eye, lse[i * 128 : (i + 1) * 128, :], 0.0)
            row = p * blocks + i
            stat_send[h, row : row + 1, :] = jnp.sum(block, axis=0, keepdims=True)

    def out_copy(h):
        where = pl.ds(pl.multiple_of(core * half + h * HD, HD), HD)
        keep = pltpu.make_async_copy(
            final.at[h, span(core), :], out_hbm.at[0, :, where], out_own.at[h]
        )
        give = pltpu.make_async_remote_copy(
            src_ref=final.at[h, span(1 - core), :], dst_ref=out_hbm.at[0, :, where],
            send_sem=out_send.at[h], recv_sem=out_recv.at[h],
            device_id={"seq": sibling}, device_id_type=MESH,
        )
        return keep, give

    def blend(h, start, size, theirs, other):
        part = slice(start, start + size)
        index = start + lax.broadcasted_iota(jnp.int32, (size, HD), 0)
        gap = jnp.where(in_cross(index), local_lse[h, part, :] - other, 200.0)
        share = 1.0 / (1.0 + jnp.exp2(jnp.minimum(gap, 100.0)))
        share = jnp.where(gap > 99.0, 0.0, share)
        mine = local_out[h, part, :]
        final[h, part, :] = (mine + share * (theirs - mine)).astype(jnp.bfloat16)

    def combine(h, p):
        for i in range(p * blocks, (p + 1) * blocks):
            line = jnp.broadcast_to(stat_recv[h, i : i + 1, :], (128, 128))
            other = jnp.sum(jnp.where(eye, line, 0.0), axis=1, keepdims=True)
            theirs = recv[h + 2, i * 128 : (i + 1) * 128, :].astype(jnp.float32)
            blend(h, i * 128, 128, theirs, other)

    def close(h):
        for copy in out_copy(h):
            copy.start()
        sums[:, column(h)] = jnp.dot(onehot, final[h], preferred_element_type=jnp.float32)

    def early_in(t, c):
        part = recv.at[t, c * tok : (c + 1) * tok, :]
        pltpu.make_async_remote_copy(
            src_ref=part, dst_ref=part,
            send_sem=early_send.at[t, 0], recv_sem=early_recv.at[t, c],
            device_id={"seq": partner}, device_id_type=MESH,
        ).wait_recv()

    def step(h, source, at, opening=False):
        for p in range(pieces):
            if not opening:
                message(h, p).wait_recv()
            elif p * PIECE % tok == 0:
                early_in(h, p * PIECE // tok)
            remote(h, p, source, at)
        stats(h).start()
        for p in range(pieces):
            local(h, p)
        if not opening:
            settle(h - 2)

    def settle(h):
        stats(h).wait_recv()
        for p in range(pieces):
            combine(h, p)
        close(h)

    for i in range(3):
        own_copies[i].wait()
        sib_copies[i].wait_recv()
    end = heads - 1
    step(0, q_all, 2, opening=True)
    step(1, q_all, 3, opening=True)

    def middle(h, carry):
        step(h, q_all, h + 2)
        return carry

    lax.fori_loop(2, heads - 3, middle, 0)
    step(heads - 3, k_all, end)
    step(heads - 2, v_all, end)
    for p in range(pieces):
        local(end, p)

    def sum_copy(n, i, other, begin, end):
        return pltpu.make_async_remote_copy(
            src_ref=sums.at[:, begin * HD : end * HD],
            dst_ref=peer_sums.at[i, :, begin * HD : end * HD],
            send_sem=sum_send.at[n, i], recv_sem=sum_recv.at[n, i],
            device_id={"seq": other}, device_id_type=MESH,
        )

    sum_copies = [
        [sum_copy(n, i, other, *cut) for i, other in enumerate((partner, diagonal, sibling))]
        for n, cut in enumerate(((0, heads - 2), (heads - 2, heads)))
    ]
    for p in range(pieces):
        message(end, p).wait_recv()
    for p in range(pieces):
        expo, top = expo_of(q_all[part_of(p), column(end)], recv[end], other_bias)
        expo_last[part_of(p), :] = expo
        top_last[part_of(p), :] = jnp.broadcast_to(top, (PIECE, HD))
    settle(end - 2)
    for copy in sum_copies[0]:
        copy.start()

    for p in range(pieces):
        message(heads, p).wait_recv()
    for p in range(pieces):
        part = part_of(p)
        theirs, other = weigh(expo_last[part, :], top_last[part, :], recv[heads])
        blend(end, p * PIECE, PIECE, theirs, other)
    close(end)
    settle(end - 1)
    for copy in sum_copies[1]:
        copy.start()

    for copy in sib_copies + early_copies:
        copy.wait_send()

    def finish_message(h, carry):
        for p in range(pieces):
            message(h + 2, p).wait_send()
        stats(h).wait_send()
        return carry

    def finish_head(h, carry):
        keep, give = out_copy(h)
        keep.wait()
        give.wait_send()
        give.wait_recv()
        return carry

    lax.fori_loop(0, end, finish_message, 0)
    lax.fori_loop(0, heads, finish_head, 0)
    for copy in sum_copies[0] + sum_copies[1]:
        copy.wait()
    here = sums[...] + peer_sums[0]
    there = peer_sums[1] + peer_sums[2]
    square = jnp.sum(here * here, axis=1, keepdims=True) + jnp.sum(
        there * there, axis=1, keepdims=True
    )
    root = jnp.sqrt(square / (2 * half) + 1e-06)
    dv_ref[0, :, group(core)] = here / root
    dv_ref[0, :, group(1 - core)] = there / root


PIECE = 256
LIMIT = 65536 - 1280


def two_chips(queries, keys, values, lengths):
    _, tok, width = queries.shape
    rows, half, docs = 2 * tok, width // 2, lengths.shape[1]
    heads = half // HD
    bf, f32 = jnp.bfloat16, jnp.float32
    dma = pltpu.SemaphoreType.DMA
    hbm = pl.BlockSpec(memory_space=pl.ANY)
    return pl.pallas_call(
        pair_kernel,
        out_shape=(
            jax.ShapeDtypeStruct(queries.shape, bf),
            jax.ShapeDtypeStruct((1, docs, width), f32),
        ),
        in_specs=[hbm, hbm, hbm, hbm],
        out_specs=(hbm, pl.BlockSpec(memory_space=pltpu.VMEM)),
        scratch_shapes=[
            pltpu.SMEM(lengths.shape, jnp.int32),
            pltpu.VMEM((rows, half), bf),
            pltpu.VMEM((rows, half), bf),
            pltpu.VMEM((rows, half), bf),
            pltpu.VMEM((rows, rows), f32),
            pltpu.VMEM((heads + 1, rows, HD), bf),
            pltpu.VMEM((heads + 1, rows, HD), bf),
            pltpu.VMEM((heads, max(rows // 128, 8), 128), f32),
            pltpu.VMEM((heads, max(rows // 128, 8), 128), f32),
            pltpu.VMEM((heads, rows, HD), f32),
            pltpu.VMEM((heads, rows, HD), f32),
            pltpu.VMEM((heads, rows, HD), bf),
            pltpu.VMEM((rows, rows), bf),
            pltpu.VMEM((rows, HD), f32),
            pltpu.VMEM((docs, half), f32),
            pltpu.VMEM((3, docs, half), f32),
            dma, dma((3,)), dma((3,)), dma((3,)), dma((2, 2)), dma((2, 2)),
            dma((heads + 1, rows // PIECE)), dma((heads + 1, rows // PIECE)),
            dma((heads,)), dma((heads,)),
            dma((heads,)), dma((heads,)), dma((heads,)),
            dma((2, 3)), dma((2, 3)),
        ],
        compiler_params=pltpu.CompilerParams(
            collective_id=0, has_side_effects=True, vmem_limit_bytes=LIMIT * 1024
        ),
        cost_estimate=pl.CostEstimate(
            flops=8 * heads * rows * rows * HD, bytes_accessed=8 * tok * width,
            transcendentals=2 * heads * rows * rows,
        ),
    )(lengths, queries, keys, values)


def per_device(queries, keys, values, lengths):
    if lax.axis_size("seq") == 4:
        return two_chips(queries, keys, values, lengths)
    return any_axis(queries, keys, values, lengths)


def solution(mesh):
    return jax.shard_map(
        per_device,
        mesh=mesh,
        in_specs=(
            P(("rep", "dp"), "seq", None),
            P(("rep", "dp"), "seq", None),
            P(("rep", "dp"), "seq", None),
            P(("rep", "dp"), None),
        ),
        out_specs=(P(("rep", "dp"), "seq", None), P(("rep", "dp"), None, None)),
        check_vma=False,
    )
```

```python
import jax
import jax.numpy as jnp
from jax import lax
from jax.experimental import pallas as pl
from jax.experimental.pallas import tpu as pltpu
from jax.sharding import PartitionSpec as P

HEADS = 16
HD = 128


def doc_index(lens, positions):
    ends = jnp.cumsum(lens)
    return jnp.sum((ends[None, :] <= positions[:, None]).astype(jnp.int32), axis=1)


def attend(queries_h, keys_h, values_h, doc_ids):
    stream = queries_h.shape[0]
    block = 512
    count = stream // block
    scale = 1.0 / queries_h.shape[2] ** 0.5

    def one_block(index):
        start = index * block
        q_block = lax.dynamic_slice_in_dim(queries_h, start, block, 0)
        ids = lax.dynamic_slice_in_dim(doc_ids, start, block, 0)
        scores = (
            jnp.einsum("qhd,khd->hqk", q_block, keys_h, preferred_element_type=jnp.float32) * scale
        )
        same = ids[:, None] == doc_ids[None, :]
        scores = jnp.where(same[None], scores, -1e30)
        top = jnp.max(scores, axis=2, keepdims=True)
        expo = jnp.exp(scores - top)
        probs = expo / jnp.sum(expo, axis=2, keepdims=True)
        weights = probs.astype(jnp.bfloat16)
        mixed = jnp.einsum("hqk,khd->qhd", weights, values_h, preferred_element_type=jnp.float32)
        return mixed.astype(jnp.bfloat16)

    out = lax.map(one_block, jnp.arange(count, dtype=jnp.int32))
    return out.reshape(stream, queries_h.shape[1], queries_h.shape[2])


def normalize(sums):
    return sums / jnp.sqrt(jnp.mean(sums * sums, axis=-1, keepdims=True) + 1e-06)


def any_axis(queries, keys, values, lengths):
    members = lax.axis_size("seq")
    tok_rows = queries.shape[1]
    width = queries.shape[2]
    local_heads = HEADS // members
    group_width = local_heads * HD
    stream = tok_rows * members
    lens = lengths[0]
    doc_count = lens.shape[0]
    q_split = queries[0].reshape(tok_rows, members, group_width)
    k_split = keys[0].reshape(tok_rows, members, group_width)
    v_split = values[0].reshape(tok_rows, members, group_width)
    q_heads, k_heads, v_heads = (
        lax.all_to_all(q_split, "seq", split_axis=1, concat_axis=0, tiled=True),
        lax.all_to_all(k_split, "seq", split_axis=1, concat_axis=0, tiled=True),
        lax.all_to_all(v_split, "seq", split_axis=1, concat_axis=0, tiled=True),
    )
    all_ids = doc_index(lens, jnp.arange(stream, dtype=jnp.int32))
    head_out = attend(
        q_heads.reshape(stream, local_heads, HD),
        k_heads.reshape(stream, local_heads, HD),
        v_heads.reshape(stream, local_heads, HD),
        all_ids,
    )
    head_rows = head_out.reshape(stream, 1, group_width)
    back = lax.all_to_all(head_rows, "seq", split_axis=0, concat_axis=1, tiled=True)
    rows = back.reshape(tok_rows, width)
    doc_range = jnp.arange(doc_count, dtype=jnp.int32)
    start = lax.axis_index("seq") * tok_rows
    local_ids = doc_index(lens, start + jnp.arange(tok_rows, dtype=jnp.int32))
    onehot_local = (local_ids[None, :] == doc_range[:, None]).astype(jnp.bfloat16)
    token_part = jnp.dot(onehot_local, rows, preferred_element_type=jnp.float32)
    sums = lax.psum(token_part, "seq")
    return (rows.reshape(1, tok_rows, width), normalize(sums).reshape(1, doc_count, width))


NEG = -1e30
LOG2E = 1.4426950408889634
MESH = pl.DeviceIdType.MESH


def pair_kernel(
    lens_hbm, q_hbm, k_hbm, v_hbm, out_hbm, dv_ref,
    lens, q_all, k_all, v_all, bias, send, recv, stat_send, stat_recv,
    local_out, local_lse, final, expo_last, top_last, sums, peer_sums,
    lens_sem, own_sem, sib_send, sib_recv, early_send, early_recv, msg_send, msg_recv,
    st_send, st_recv, out_own, out_send, out_recv, sum_send, sum_recv,
):
    me = lax.axis_index("seq")
    chip = me // 2
    core = lax.rem(me, 2)
    sibling = chip * 2 + 1 - core
    partner = (1 - chip) * 2 + core
    diagonal = (1 - chip) * 2 + 1 - core
    tok = q_hbm.shape[1]
    rows = 2 * tok
    half = q_hbm.shape[2] // 2
    heads = half // HD
    docs = lens.shape[1]
    factor = LOG2E / HD**0.5
    pieces = rows // PIECE
    blocks = PIECE // 128

    def column(h):
        return pl.ds(pl.multiple_of(h * HD, HD), HD)

    def group(g):
        return pl.ds(pl.multiple_of(g * half, half), half)

    def span(c):
        return pl.ds(pl.multiple_of(c * tok, tok), tok)

    lens_copy = pltpu.make_async_copy(lens_hbm, lens, lens_sem)
    lens_copy.start()
    own_copies = [
        pltpu.make_async_copy(src.at[0, :, group(core)], dst.at[span(core), :], own_sem.at[i])
        for i, (src, dst) in enumerate(((k_hbm, k_all), (v_hbm, v_all), (q_hbm, q_all)))
    ]
    for copy in own_copies:
        copy.start()

    barrier = pltpu.get_barrier_semaphore()
    for other in (sibling, partner, diagonal):
        pl.semaphore_signal(barrier, inc=1, device_id={"seq": other}, device_id_type=MESH)
    pl.semaphore_wait(barrier, 3)

    def early(t, i, there, g):
        return pltpu.make_async_remote_copy(
            src_ref=q_hbm.at[0, :, pl.ds(pl.multiple_of(g * half + t * HD, HD), HD)],
            dst_ref=recv.at[t, span(core), :],
            send_sem=early_send.at[t, i], recv_sem=early_recv.at[t, core],
            device_id={"seq": there}, device_id_type=MESH,
        )

    early_copies = [
        early(t, i, *to) for t in range(2) for i, to in enumerate(((partner, core), (diagonal, 1 - core)))
    ]
    for copy in early_copies:
        copy.start()
    sib_copies = [
        pltpu.make_async_remote_copy(
            src_ref=src.at[0, :, group(1 - core)], dst_ref=dst.at[span(core), :],
            send_sem=sib_send.at[i], recv_sem=sib_recv.at[i],
            device_id={"seq": sibling}, device_id_type=MESH,
        )
        for i, (src, dst) in enumerate(((k_hbm, k_all), (v_hbm, v_all), (q_hbm, q_all)))
    ]
    for copy in sib_copies:
        copy.start()

    lens_copy.wait()
    ends = []
    total = jnp.int32(0)
    for j in range(docs):
        total = total + lens[0, j]
        ends.append(total)
    first = jnp.int32(0)
    last = jnp.int32(2 * rows)
    for end in ends:
        first = jnp.maximum(first, jnp.where(end <= rows, end, 0))
        last = jnp.minimum(last, jnp.where(end > rows, end, 2 * rows))
    low = jnp.where(chip == 0, first, 0)
    high = jnp.where(chip == 0, rows, last - rows)

    other_low = jnp.where(chip == 0, 0, first)
    other_high = jnp.where(chip == 0, last - rows, rows)

    def in_cross(index):
        return (index >= low) & (index < high)

    def ids_of(index):
        ids = jnp.zeros(index.shape, jnp.int32)
        for end in ends:
            ids = ids + (end <= index).astype(jnp.int32)
        return ids

    lane_pos = lax.broadcasted_iota(jnp.int32, (1, rows), 1)
    lane_ids = ids_of(lane_pos + chip * rows)
    sub_ids = ids_of(lax.broadcasted_iota(jnp.int32, (rows, 1), 0) + chip * rows)
    bias[...] = jnp.where(sub_ids == lane_ids, 0.0, NEG)
    cross_bias = jnp.where(in_cross(lane_pos), 0.0, NEG)
    other_bias = jnp.where((lane_pos >= other_low) & (lane_pos < other_high), 0.0, NEG)
    onehot = (lane_ids == lax.broadcasted_iota(jnp.int32, (docs, rows), 0)).astype(jnp.bfloat16)
    eye = lax.broadcasted_iota(jnp.int32, (128, 128), 0) == lax.broadcasted_iota(
        jnp.int32, (128, 128), 1
    )
    ones = jnp.ones((rows, HD), jnp.bfloat16)

    def part_of(p):
        return slice(p * PIECE, (p + 1) * PIECE)

    def message(t, p):
        return pltpu.make_async_remote_copy(
            src_ref=send.at[t, part_of(p), :], dst_ref=recv.at[t, part_of(p), :],
            send_sem=msg_send.at[t, p], recv_sem=msg_recv.at[t, p],
            device_id={"seq": partner}, device_id_type=MESH,
        )

    def stats(h):
        return pltpu.make_async_remote_copy(
            src_ref=stat_send.at[h], dst_ref=stat_recv.at[h],
            send_sem=st_send.at[h], recv_sem=st_recv.at[h],
            device_id={"seq": partner}, device_id_type=MESH,
        )

    def expo_of(q, keys, bias_rows):
        scores = lax.dot_general(
            q, keys, (((1,), (1,)), ((), ())), preferred_element_type=jnp.float32
        )
        scores = scores * factor + bias_rows
        top = jnp.max(scores, axis=1, keepdims=True)
        return jnp.exp2(scores - top).astype(jnp.bfloat16), top

    def weigh(expo, top, vals):
        wide = jnp.concatenate([vals, ones], axis=1)
        both = jnp.dot(expo, wide, preferred_element_type=jnp.float32)
        mass = both[:, HD:]
        return both[:, :HD] / mass, top + jnp.log2(mass)

    def mix(q, h, bias_rows):
        expo, top = expo_of(q, k_all[:, column(h)], bias_rows)
        return weigh(expo, top, v_all[:, column(h)])

    def local(h, p):
        part = part_of(p)
        out, lse = mix(q_all[part, column(h)], h, bias[part, :])
        local_out[h, part, :] = out
        local_lse[h, part, :] = lse

    def remote(h, p, source, at):
        part = part_of(p)
        out, lse = mix(recv[h, part, :], h, cross_bias)
        index = p * PIECE + lax.broadcasted_iota(jnp.int32, (PIECE, HD), 0)
        own = source[part, column(at)].astype(jnp.float32)
        send[h + 2, part, :] = jnp.where(in_cross(index), own, out).astype(jnp.bfloat16)
        message(h + 2, p).start()
        for i in range(blocks):
            block = jnp.where(eye, lse[i * 128 : (i + 1) * 128, :], 0.0)
            row = p * blocks + i
            stat_send[h, row : row + 1, :] = jnp.sum(block, axis=0, keepdims=True)

    def out_copy(h):
        where = pl.ds(pl.multiple_of(core * half + h * HD, HD), HD)
        keep = pltpu.make_async_copy(
            final.at[h, span(core), :], out_hbm.at[0, :, where], out_own.at[h]
        )
        give = pltpu.make_async_remote_copy(
            src_ref=final.at[h, span(1 - core), :], dst_ref=out_hbm.at[0, :, where],
            send_sem=out_send.at[h], recv_sem=out_recv.at[h],
            device_id={"seq": sibling}, device_id_type=MESH,
        )
        return keep, give

    def blend(h, start, size, theirs, other):
        part = slice(start, start + size)
        index = start + lax.broadcasted_iota(jnp.int32, (size, HD), 0)
        gap = jnp.where(in_cross(index), local_lse[h, part, :] - other, 200.0)
        share = 1.0 / (1.0 + jnp.exp2(jnp.minimum(gap, 100.0)))
        share = jnp.where(gap > 99.0, 0.0, share)
        mine = local_out[h, part, :]
        final[h, part, :] = (mine + share * (theirs - mine)).astype(jnp.bfloat16)

    def combine(h, p):
        for i in range(p * blocks, (p + 1) * blocks):
            line = jnp.broadcast_to(stat_recv[h, i : i + 1, :], (128, 128))
            other = jnp.sum(jnp.where(eye, line, 0.0), axis=1, keepdims=True)
            theirs = recv[h + 2, i * 128 : (i + 1) * 128, :].astype(jnp.float32)
            blend(h, i * 128, 128, theirs, other)

    def close(h):
        for copy in out_copy(h):
            copy.start()
        sums[:, column(h)] = jnp.dot(onehot, final[h], preferred_element_type=jnp.float32)

    def early_in(t, c):
        part = recv.at[t, c * tok : (c + 1) * tok, :]
        pltpu.make_async_remote_copy(
            src_ref=part, dst_ref=part,
            send_sem=early_send.at[t, 0], recv_sem=early_recv.at[t, c],
            device_id={"seq": partner}, device_id_type=MESH,
        ).wait_recv()

    def step(h, source, at, opening=False):
        for p in range(pieces):
            if not opening:
                message(h, p).wait_recv()
            elif p * PIECE % tok == 0:
                early_in(h, p * PIECE // tok)
            remote(h, p, source, at)
        stats(h).start()
        for p in range(pieces):
            local(h, p)
        if not opening:
            settle(h - 2)

    def settle(h):
        stats(h).wait_recv()
        for p in range(pieces):
            combine(h, p)
        close(h)

    for i in range(3):
        own_copies[i].wait()
        sib_copies[i].wait_recv()
    end = heads - 1
    step(0, q_all, 2, opening=True)
    step(1, q_all, 3, opening=True)

    def middle(h, carry):
        step(h, q_all, h + 2)
        return carry

    lax.fori_loop(2, heads - 3, middle, 0)
    step(heads - 3, k_all, end)
    step(heads - 2, v_all, end)
    for p in range(pieces):
        local(end, p)

    def sum_copy(n, i, other, begin, end):
        return pltpu.make_async_remote_copy(
            src_ref=sums.at[:, begin * HD : end * HD],
            dst_ref=peer_sums.at[i, :, begin * HD : end * HD],
            send_sem=sum_send.at[n, i], recv_sem=sum_recv.at[n, i],
            device_id={"seq": other}, device_id_type=MESH,
        )

    sum_copies = [
        [sum_copy(n, i, other, *cut) for i, other in enumerate((partner, diagonal, sibling))]
        for n, cut in enumerate(((0, heads - 2), (heads - 2, heads)))
    ]
    for p in range(pieces):
        message(end, p).wait_recv()
    for p in range(pieces):
        expo, top = expo_of(q_all[part_of(p), column(end)], recv[end], other_bias)
        expo_last[part_of(p), :] = expo
        top_last[part_of(p), :] = jnp.broadcast_to(top, (PIECE, HD))
    settle(end - 2)
    for copy in sum_copies[0]:
        copy.start()

    for p in range(pieces):
        message(heads, p).wait_recv()
    for p in range(pieces):
        part = part_of(p)
        theirs, other = weigh(expo_last[part, :], top_last[part, :], recv[heads])
        blend(end, p * PIECE, PIECE, theirs, other)
    close(end)
    settle(end - 1)
    for copy in sum_copies[1]:
        copy.start()

    for copy in sib_copies + early_copies:
        copy.wait_send()

    def finish_message(h, carry):
        for p in range(pieces):
            message(h + 2, p).wait_send()
        stats(h).wait_send()
        return carry

    def finish_head(h, carry):
        keep, give = out_copy(h)
        keep.wait()
        give.wait_send()
        give.wait_recv()
        return carry

    lax.fori_loop(0, end, finish_message, 0)
    lax.fori_loop(0, heads, finish_head, 0)
    for copy in sum_copies[0] + sum_copies[1]:
        copy.wait()
    here = sums[...] + peer_sums[0]
    there = peer_sums[1] + peer_sums[2]
    square = jnp.sum(here * here, axis=1, keepdims=True) + jnp.sum(
        there * there, axis=1, keepdims=True
    )
    root = jnp.sqrt(square / (2 * half) + 1e-06)
    dv_ref[0, :, group(core)] = here / root
    dv_ref[0, :, group(1 - core)] = there / root


PIECE = 256
SHARES = 4
LIMIT = 65536 - 128


def hand_over(rows_in, vec_in, rows_out, vec_out, rows_held, vec_held, sems_in, sems_out):
    share = rows_in.shape[1] // SHARES
    legs = []
    for i in range(SHARES):
        part = slice(i * share, (i + 1) * share)
        held = rows_held.at[:, part, :]
        legs.append((rows_in.at[:, part, :], held, rows_out.at[:, part, :]))
    legs.append((vec_in, vec_held, vec_out))
    ins = [pltpu.make_async_copy(a, b, sems_in.at[i]) for i, (a, b, c) in enumerate(legs)]
    outs = [pltpu.make_async_copy(b, c, sems_out.at[i]) for i, (a, b, c) in enumerate(legs)]
    for copy in ins:
        copy.start()
    for arrive, leave in zip(ins, outs):
        arrive.wait()
        leave.start()
    for copy in outs:
        copy.wait()


def two_chips(queries, keys, values, lengths):
    _, tok, width = queries.shape
    rows, half, docs = 2 * tok, width // 2, lengths.shape[1]
    heads = half // HD
    bf, f32 = jnp.bfloat16, jnp.float32
    dma = pltpu.SemaphoreType.DMA
    hbm = pl.BlockSpec(memory_space=pl.ANY)
    attended, vectors = pl.pallas_call(
        pair_kernel,
        out_shape=(
            jax.ShapeDtypeStruct(queries.shape, bf),
            jax.ShapeDtypeStruct((1, docs, width), f32),
        ),
        in_specs=[hbm, hbm, hbm, hbm],
        out_specs=(hbm, pl.BlockSpec(memory_space=pltpu.VMEM)),
        scratch_shapes=[
            pltpu.SMEM(lengths.shape, jnp.int32),
            pltpu.VMEM((rows, half), bf),
            pltpu.VMEM((rows, half), bf),
            pltpu.VMEM((rows, half), bf),
            pltpu.VMEM((rows, rows), f32),
            pltpu.VMEM((heads + 1, rows, HD), bf),
            pltpu.VMEM((heads + 1, rows, HD), bf),
            pltpu.VMEM((heads, max(rows // 128, 8), 128), f32),
            pltpu.VMEM((heads, max(rows // 128, 8), 128), f32),
            pltpu.VMEM((heads, rows, HD), f32),
            pltpu.VMEM((heads, rows, HD), f32),
            pltpu.VMEM((heads, rows, HD), bf),
            pltpu.VMEM((rows, rows), bf),
            pltpu.VMEM((rows, HD), f32),
            pltpu.VMEM((docs, half), f32),
            pltpu.VMEM((3, docs, half), f32),
            dma, dma((3,)), dma((3,)), dma((3,)), dma((2, 2)), dma((2, 2)),
            dma((heads + 1, rows // PIECE)), dma((heads + 1, rows // PIECE)),
            dma((heads,)), dma((heads,)),
            dma((heads,)), dma((heads,)), dma((heads,)),
            dma((2, 3)), dma((2, 3)),
        ],
        compiler_params=pltpu.CompilerParams(
            collective_id=0, has_side_effects=True, vmem_limit_bytes=LIMIT * 1024
        ),
        cost_estimate=pl.CostEstimate(
            flops=8 * heads * rows * rows * HD, bytes_accessed=8 * tok * width,
            transcendentals=2 * heads * rows * rows,
        ),
    )(lengths, queries, keys, values)
    return pl.pallas_call(
        hand_over,
        out_shape=(
            jax.ShapeDtypeStruct(attended.shape, bf),
            jax.ShapeDtypeStruct(vectors.shape, f32),
        ),
        in_specs=[hbm, hbm],
        out_specs=(hbm, hbm),
        scratch_shapes=[
            pltpu.VMEM(attended.shape, bf),
            pltpu.VMEM(vectors.shape, f32),
            dma((SHARES + 1,)),
            dma((SHARES + 1,)),
        ],
        cost_estimate=pl.CostEstimate(flops=0, bytes_accessed=4 * tok * width, transcendentals=0),
    )(attended, vectors)


def per_device(queries, keys, values, lengths):
    if lax.axis_size("seq") == 4:
        return two_chips(queries, keys, values, lengths)
    return any_axis(queries, keys, values, lengths)


def solution(mesh):
    return jax.shard_map(
        per_device,
        mesh=mesh,
        in_specs=(
            P(("rep", "dp"), "seq", None),
            P(("rep", "dp"), "seq", None),
            P(("rep", "dp"), "seq", None),
            P(("rep", "dp"), None),
        ),
        out_specs=(P(("rep", "dp"), "seq", None), P(("rep", "dp"), None, None)),
        check_vma=False,
    )
```
